512 devices in a mesh: ctx: 64 (over y, x, core), tp: 8 (over z).
Axes of the slice: x: 4, y: 8, z: 8, core: 2. Of those that a mesh axis runs over, the one named last changes fastest.
Arguments:
- mamba_input: bfloat16 [8192, 8192], P('ctx', 'tp'), may hold values from -6 to 6
- step: float32 [8192, 128], P('ctx', 'tp'), may hold values from 0.5 to 2
- log_decay: float32 [8192, 128], P('ctx', 'tp'), may hold values from -0.75 to 0
- state_in: bfloat16 [8192, 8, 256], P('ctx', 'tp'), may hold values from -0.0625 to 0.0625
- state_out: bfloat16 [8192, 8, 256], P('ctx', 'tp'), may hold values from -6 to 6
- skip_gain: float32 [128], P('tp'), may hold values from 0.5 to 1.5
- queries: bfloat16 [8192, 4096], P('ctx', 'tp'), may hold values from -120 to 120
- keys: bfloat16 [8192, 1024], P('ctx', 'tp'), may hold values from -6 to 6
- values: bfloat16 [8192, 1024], P('ctx', 'tp'), may hold values from -6 to 6
- residual: bfloat16 [8192, 8192], P('ctx', 'tp'), may hold values from -240 to 240
- norm_gain: float32 [8192], P('tp'), may hold values from 0.5 to 1.5
Outputs:
- mamba_out: bfloat16 [8192, 8192], P('ctx', 'tp')
- attn_out: bfloat16 [8192, 4096], P('ctx', 'tp')
- normed: bfloat16 [8192, 8192], P('ctx', 'tp')
The draws below stay inside these ranges and needn't reach their ends.
All inputs are finite; a program needn't handle non-finite values.
Results may differ from the reference program's by a relative error of at most 0.009.
Values may be sent and summed in bfloat16 or wider, within the bound.
No kernel may reach another device: no remote copies, remote signals or barrier semaphores. Data moves between devices by JAX's collectives and lax.ppermute only.
A program may use at most 192 MiB of HBM per device.

```python
import math
import jax
import jax.numpy as jnp
from jax import lax

D = 8192
MDIM = 64
SDIM = 256
GR = 8
MAMBA_HEADS = 128
SCAN_BLOCK_SIZE = 128
QUERY_HEADS = 32
KEY_VALUE_HEADS = 8
HEAD_SIZE = 128
SEQUENCE_LENGTH = 8192


def base_keys(key):
    return jnp.clip(jax.random.normal(key, (SEQUENCE_LENGTH, KEY_VALUE_HEADS * HEAD_SIZE), jnp.float32), -5.5, 5.5)


def draw_keys(key, part):
    shared_heads = base_keys(key)
    return shared_heads.astype(jnp.bfloat16)


def draw_queries(key, part):
    key = jax.random.fold_in(key, 3)
    fresh = jnp.clip(jax.random.normal(key, (SEQUENCE_LENGTH, QUERY_HEADS * HEAD_SIZE), jnp.float32), -5.5, 5.5)
    return fresh.astype(jnp.bfloat16)


def draw_log_decay(key, part):
    key = jax.random.fold_in(key, 5)
    key_frequency, key_jitter, key_position, key_spike = jax.random.split(key, 4)
    upper_log = math.log(0.03)
    lower_log = math.log(0.01 / SEQUENCE_LENGTH)
    rates = jnp.exp(jax.random.uniform(key_frequency, (MAMBA_HEADS,), jnp.float32, lower_log, upper_log))
    roughness = jnp.exp(jax.random.uniform(key_jitter, (SEQUENCE_LENGTH, MAMBA_HEADS), jnp.float32, math.log(0.5), math.log(2.0)))
    spike_events = jax.random.randint(key_position, (6,), 0, SEQUENCE_LENGTH)
    spike_hits = jnp.any(jnp.arange(SEQUENCE_LENGTH)[:, None] == spike_events[None, :], axis=1)
    sudden_jumps = jax.random.uniform(key_spike, (SEQUENCE_LENGTH, MAMBA_HEADS), jnp.float32, 0.25, 0.65)
    return -(rates[None, :] * roughness + jnp.where(spike_hits[:, None], sudden_jumps, 0.0))


def draw_residual(key, part):
    key = jax.random.fold_in(key, 7)
    key_base, key_cols, key_matrix = jax.random.split(key, 3)
    columns = jnp.arange(D).astype(jnp.float32)
    rise = jnp.exp(math.log(10.0) * columns / D)
    column_rough = jnp.exp(jax.random.uniform(key_cols, (D,), jnp.float32, math.log(0.5), math.log(2.0)))
    row_scale = jnp.exp(jax.random.uniform(key_matrix, (SEQUENCE_LENGTH,), jnp.float32, 0.0, math.log(10.0)))
    base = jnp.clip(jax.random.normal(key_base, (SEQUENCE_LENGTH, D), jnp.float32), -5.5, 5.5)
    return (0.2 * base * row_scale[:, None] * rise[None, :] * column_rough[None, :]).astype(jnp.bfloat16)


def level_of(key, extent, cuts, smallest, high):
    def one(position, parts):
        heights = jax.random.uniform(jax.random.fold_in(jax.random.fold_in(key, 6), position), (parts,), jnp.float32, smallest / len(cuts), high / len(cuts))
        return jnp.repeat(jnp.exp(heights), extent[position] // parts).reshape((-1,) + (1,) * (len(extent) - position - 1))

    loudness = one(*cuts[0])
    for cut in cuts[1:]:
        loudness = loudness * one(*cut)
    return loudness


def scatter_about(rng, extent, width, reach, cuts=(), held_as=jnp.bfloat16):
    array = jax.random.normal(rng, extent, jnp.float32) * width
    if len(cuts) > 0:
        array = level_of(rng, extent, cuts, -0.22, 0.18) * array
    return jnp.clip(array, min=-reach, max=reach).astype(held_as)


def setup_inputs(seed: int = 0) -> dict:
    key_of = jax.random.split(jax.random.key(seed), 12)
    mamba_input = scatter_about(key_of[0], (SEQUENCE_LENGTH, MAMBA_HEADS * MDIM), 1.0, 6.0, ((0, 64), (1, 8)))
    step = jnp.clip(jnp.exp(math.log(2.0) - 1.3862944 * jax.random.uniform(key_of[1], (SEQUENCE_LENGTH, MAMBA_HEADS), jnp.float32) ** level_of(key_of[1], (SEQUENCE_LENGTH, MAMBA_HEADS), ((0, 64), (1, 8)), -0.2, 0.2)), 0.5, 2.0)
    log_decay = draw_log_decay(jax.random.fold_in(key_of[11], 71), 0)
    state_in = scatter_about(key_of[3], (SEQUENCE_LENGTH, GR, SDIM), ((SDIM * 256) ** -0.5), 0.0625, ((0, 64), (1, 8)))
    state_out = scatter_about(key_of[4], (SEQUENCE_LENGTH, GR, SDIM), 1.0, 6.0, ((0, 64), (1, 8)))
    skip_gain = jnp.clip(1.0 + 0.1 * jax.random.normal(key_of[5], (MAMBA_HEADS,), jnp.float32), 0.5, 1.5)
    queries = draw_queries(jax.random.fold_in(key_of[11], 71), 0)
    keys = draw_keys(jax.random.fold_in(key_of[11], 71), 0)
    values = scatter_about(key_of[8], (SEQUENCE_LENGTH, KEY_VALUE_HEADS * HEAD_SIZE), 1.0, 6.0, ((0, 64), (1, 8)))
    residual = draw_residual(jax.random.fold_in(key_of[11], 71), 0)
    norm_gain = jnp.clip(1.0 + 0.1 * jax.random.normal(key_of[10], (D,), jnp.float32), 0.5, 1.5)
    return {"mamba_input": mamba_input, "step": step, "log_decay": log_decay, "state_in": state_in, "state_out": state_out, "skip_gain": skip_gain, "queries": queries, "keys": keys, "values": values, "residual": residual, "norm_gain": norm_gain}


def block_terms(block_in, block_step, block_decay, block_b, block_c):
    length = block_in.shape[0]
    running = jnp.cumsum(block_decay, axis=0)
    intersection = jnp.einsum('tgn,sgn->gts', block_c.astype(jnp.float32), block_b.astype(jnp.float32))
    causal = jnp.arange(length)[:, None] >= jnp.arange(length)[None, :]
    spread = jnp.transpose(running[:, None] - running[None, :], (2, 3, 0, 1))
    decays = jnp.where(causal, jnp.exp(jnp.where(causal, spread, 0.0)), 0.0)
    weight = decays * intersection[:, None] * jnp.transpose(block_step, (1, 2, 0))[:, :, None, :]
    weight = lax.optimization_barrier(weight.astype(jnp.bfloat16)).astype(jnp.float32)
    inside = jnp.einsum('gjts,sgjp->tgjp', weight, block_in.astype(jnp.float32))
    to_end = jnp.exp(running[-1][None] - running) * block_step
    scaled = (to_end[..., None] * block_in.astype(jnp.float32)).astype(jnp.bfloat16)
    scaled = lax.optimization_barrier(scaled).astype(jnp.float32)
    states = jnp.einsum('sgjp,sgn->gjpn', scaled, block_b.astype(jnp.float32))
    return (inside, states, jnp.exp(running[-1]), running)

def mamba_layer(mamba_input, step, log_decay, state_in, state_out, skip_gain):
    count = SEQUENCE_LENGTH // SCAN_BLOCK_SIZE
    heads_per_group = MAMBA_HEADS // GR
    x_in = mamba_input.reshape(count, SCAN_BLOCK_SIZE, GR, heads_per_group, MDIM)
    steps_in = step.reshape(count, SCAN_BLOCK_SIZE, GR, heads_per_group)
    decays_in = log_decay.reshape(count, SCAN_BLOCK_SIZE, GR, heads_per_group)
    b_in = state_in.reshape(count, SCAN_BLOCK_SIZE, GR, SDIM)
    c_in = state_out.reshape(count, SCAN_BLOCK_SIZE, GR, SDIM)
    gains = skip_gain.reshape(GR, heads_per_group)

    def advance(entering, pieces):
        block_x, block_step, block_decay, block_b, block_c = pieces
        inside, states, totals, running = block_terms(block_x, block_step, block_decay, block_b, block_c)
        entering_low = lax.optimization_barrier(entering.astype(jnp.bfloat16)).astype(jnp.float32)
        carried = jnp.einsum('tgn,gjpn->tgjp', block_c.astype(jnp.float32), entering_low)
        result = inside + jnp.exp(running)[..., None] * carried + gains[None, :, :, None] * block_x.astype(jnp.float32)
        return (totals[..., None, None] * entering + states, result.astype(jnp.bfloat16))
    start_state = jnp.zeros((GR, heads_per_group, MDIM, SDIM), jnp.float32)
    _, results = lax.scan(advance, start_state, (x_in, steps_in, decays_in, b_in, c_in))
    return results.reshape(SEQUENCE_LENGTH, MAMBA_HEADS * MDIM)

def attention_layer(queries, keys, values):
    heads_per_group = QUERY_HEADS // KEY_VALUE_HEADS
    query_block_list = queries.reshape(SEQUENCE_LENGTH // SCAN_BLOCK_SIZE, SCAN_BLOCK_SIZE, KEY_VALUE_HEADS, heads_per_group, HEAD_SIZE)
    key_matrix = keys.reshape(SEQUENCE_LENGTH, KEY_VALUE_HEADS, HEAD_SIZE).astype(jnp.float32)
    value_matrix = values.reshape(SEQUENCE_LENGTH, KEY_VALUE_HEADS, HEAD_SIZE).astype(jnp.float32)
    positions = jnp.arange(SEQUENCE_LENGTH).astype(jnp.int32)

    def one_block(pieces):
        q_block, block_index = pieces
        scores = jnp.einsum('rgqe,kge->gqrk', q_block.astype(jnp.float32), key_matrix) * HEAD_SIZE ** (-0.5)
        row_places = block_index * SCAN_BLOCK_SIZE + jnp.arange(SCAN_BLOCK_SIZE).astype(jnp.int32)
        visible = row_places[:, None] >= positions[None, :]
        scores = jnp.where(visible, scores, -jnp.inf)
        highest = lax.optimization_barrier(jnp.max(scores, axis=-1, keepdims=True))
        weights = jnp.where(visible, jnp.exp(scores - highest), 0.0)
        denominator = lax.optimization_barrier(jnp.sum(weights, axis=-1))
        rounded = lax.optimization_barrier(weights.astype(jnp.bfloat16)).astype(jnp.float32)
        numerator = jnp.einsum('gqrk,kge->gqre', rounded, value_matrix)
        output = numerator / denominator[..., None]
        output = jnp.transpose(output, (2, 0, 1, 3)).reshape(SCAN_BLOCK_SIZE, QUERY_HEADS * HEAD_SIZE)
        return output.astype(jnp.bfloat16)
    outputs = lax.map(one_block, (query_block_list, jnp.arange(SEQUENCE_LENGTH // SCAN_BLOCK_SIZE).astype(jnp.int32)))
    return outputs.reshape(SEQUENCE_LENGTH, QUERY_HEADS * HEAD_SIZE)

def norm_layer(residual, norm_gain):
    widened = residual.astype(jnp.float32)
    mean_square = lax.optimization_barrier(jnp.mean(widened * widened, axis=1, keepdims=True))
    return (widened * lax.rsqrt(mean_square + 1e-05) * norm_gain[None, :]).astype(jnp.bfloat16)

def reference(mamba_input, step, log_decay, state_in, state_out, skip_gain, queries, keys, values, residual, norm_gain):
    mamba_out = mamba_layer(mamba_input, step, log_decay, state_in, state_out, skip_gain)
    attn_out = attention_layer(queries, keys, values)
    normed = norm_layer(residual, norm_gain)
    return (mamba_out, attn_out, normed)
```

```python
import functools
import math

import jax
import jax.numpy as jnp
from jax import lax
from jax.experimental import pallas as pl
from jax.experimental.pallas import tpu as pltpu
from jax.sharding import Mesh, PartitionSpec as P

D = 8192
MDIM = 64
SDIM = 256
BLOCK = 128
HEAD_SIZE = 128
NY, NX, NC, NZ = 8, 4, 2, 8
CHIPS = NY * NX
HALF = 8
LOW = -1e30
F32 = jnp.float32
BF16 = jnp.bfloat16
NT = (((1,), (1,)), ((), ()))
TN = (((0,), (0,)), ((), ()))
VMEM = pl.BlockSpec(memory_space=pltpu.VMEM)
SMEM = pl.BlockSpec(memory_space=pltpu.SMEM)


def dot(a, b, dims=(((1,), (0,)), ((), ())), precision=None):
    return lax.dot_general(a, b, dims, preferred_element_type=F32, precision=precision)


def call(kernel, outs, scratch=(), cost=None, scalars=1, inputs=1):
    return pl.pallas_call(
        kernel,
        out_shape=outs,
        in_specs=[SMEM] * scalars + [VMEM] * inputs,
        out_specs=jax.tree.map(lambda _: VMEM, outs),
        scratch_shapes=list(scratch),
        compiler_params=pltpu.CompilerParams(vmem_limit_bytes=40 * 1024 * 1024),
        cost_estimate=cost,
    )


def shape(dims, dtype):
    return jax.ShapeDtypeStruct(dims, dtype)


def cost(us):
    return pl.CostEstimate(flops=int(us * 1e6 * 1000), bytes_accessed=int(us * 3e6), transcendentals=0)


def split3(v):
    hi = v.astype(BF16)
    rest = v - hi.astype(F32)
    mid = rest.astype(BF16)
    lo = (rest - mid.astype(F32)).astype(BF16)
    return hi, mid, lo


def prepare_kernel(place, x, step, decay, b, c, send, rows_send, rows_keep):
    core = place[2]
    tri = (
        lax.broadcasted_iota(jnp.int32, (BLOCK, BLOCK), 0)
        <= lax.broadcasted_iota(jnp.int32, (BLOCK, BLOCK), 1)
    ).astype(F32)
    eye = (
        lax.broadcasted_iota(jnp.int32, (BLOCK, BLOCK), 0)
        == lax.broadcasted_iota(jnp.int32, (BLOCK, BLOCK), 1)
    ).astype(F32)
    run = dot(decay[...], tri, TN, lax.Precision.HIGHEST)
    steps = dot(step[...], eye, TN, lax.Precision.HIGHEST)
    low = jnp.concatenate([run[:HALF], steps[:HALF]], axis=0)
    high = jnp.concatenate([run[HALF:], steps[HALF:]], axis=0)
    rows_keep[...] = jnp.where(core == 0, low, high)
    rows_send[...] = jnp.where(core == 0, high, low)
    send[:, :512] = jnp.where(core == 0, x[:, 512:], x[:, :512])
    send[:, 512:768] = b[...]
    send[:, 768:] = c[...]


def columns_of(rows):
    padded = jnp.concatenate([rows, jnp.zeros((BLOCK - rows.shape[0], BLOCK), F32)], axis=0)
    return padded.T


def spread(cols, first):
    lane = lax.broadcasted_iota(jnp.int32, (BLOCK, 128), 1)
    return jnp.where(lane < MDIM, cols[:, first : first + 1], cols[:, first + 1 : first + 2])


def states_kernel(place, x, b, c, rows_own, received, rows_other, gain, payload, first_state, inside):
    core = place[2]
    causal = lax.broadcasted_iota(jnp.int32, (BLOCK, BLOCK), 0) >= lax.broadcasted_iota(
        jnp.int32, (BLOCK, BLOCK), 1
    )
    x_own = jnp.where(core == 0, x[:, :512], x[:, 512:])
    blocks = (
        (x_own, b[...], c[...], rows_own[...]),
        (received[:, :512], received[:, 512:768], received[:, 768:], rows_other[...]),
    )
    gains = gain[...]
    states = []
    totals = []
    for which, (xs, bs, cs, rows) in enumerate(blocks):
        cols = columns_of(rows)
        mixed = dot(cs, bs, NT)
        ends = rows[:, BLOCK - 1 : BLOCK]
        totals.append(ends)
        scaled = []
        for pair in range(HALF // 2):
            parts = []
            for head in (2 * pair, 2 * pair + 1):
                gap = cols[:, head : head + 1] - rows[head : head + 1, :]
                grown = jnp.exp(jnp.where(causal, gap, LOW))
                weight = (grown * mixed * rows[HALF + head : HALF + head + 1, :]).astype(BF16)
                parts.append(dot(weight, xs[:, head * MDIM : (head + 1) * MDIM]))
            lanes = slice(pair * 128, (pair + 1) * 128)
            wide = xs[:, lanes].astype(F32)
            inside[which, :, lanes] = jnp.concatenate(parts, axis=1) + gains[:, lanes] * wide
            lane = lax.broadcasted_iota(jnp.int32, (1, 128), 1)
            end = jnp.where(lane < MDIM, ends[2 * pair : 2 * pair + 1], ends[2 * pair + 1 : 2 * pair + 2])
            to_end = jnp.exp(end - spread(cols, 2 * pair)) * spread(cols, HALF + 2 * pair)
            scaled.append((to_end * wide).astype(BF16))
        states.append(dot(jnp.concatenate(scaled, axis=1), bs, TN))
    lengths = totals[0] + totals[1]
    for head in range(HALF):
        rows = slice(head * MDIM, (head + 1) * MDIM)
        own, other = states[0][rows], states[1][rows]
        gain_own = jnp.exp(totals[0][head : head + 1])
        gain_other = jnp.exp(totals[1][head : head + 1])
        first_state[rows, :] = jnp.where(core == 0, own, other)
        joint = jnp.where(core == 0, gain_other * own + other, gain_own * other + own).astype(BF16)
        hi, mid, lo = split3(jnp.broadcast_to(lengths[head : head + 1], (8, 128)))
        tag = lax.broadcasted_iota(jnp.int32, (8, 128), 0)
        total = jnp.where(tag == 0, hi.astype(F32), jnp.where(tag == 1, mid.astype(F32), lo.astype(F32)))
        for part in range(4):
            chunk = head * 4 + part
            payload[chunk, 0:16, :] = joint[part * 16 : (part + 1) * 16, :128]
            payload[chunk, 16:32, :] = joint[part * 16 : (part + 1) * 16, 128:]
            payload[chunk, 32:40, :] = total.astype(BF16)


def scan_kernel(arrived, entering):
    state = jnp.zeros((32, 128), F32)
    for chip in range(CHIPS):
        entering[chip] = state.astype(BF16)
        tail = arrived[chip, 32:40, :].astype(F32)
        gain = jnp.exp(tail[0:1] + tail[1:2] + tail[2:3])
        state = gain * state + arrived[chip, 0:32, :].astype(F32)


def finish_kernel(place, entering, first_state, inside, c, received, rows_own, rows_other, own, other):
    core = place[2]
    state_low = entering[:, 0:16, :].reshape(512, 128)
    state_high = entering[:, 16:32, :].reshape(512, 128)
    rows_mine, rows_theirs = rows_own[...], rows_other[...]
    first_total = jnp.where(core == 0, rows_mine[:HALF], rows_theirs[:HALF])[:, BLOCK - 1 : BLOCK]
    gain = jnp.exp(first_total)
    low, high = [], []
    for head in range(HALF):
        rows = slice(head * MDIM, (head + 1) * MDIM)
        low.append(gain[head : head + 1] * state_low[rows].astype(F32) + first_state[rows, :128])
        high.append(gain[head : head + 1] * state_high[rows].astype(F32) + first_state[rows, 128:])
    next_low = jnp.concatenate(low, axis=0).astype(BF16)
    next_high = jnp.concatenate(high, axis=0).astype(BF16)
    own_low = jnp.where(core == 0, state_low, next_low)
    own_high = jnp.where(core == 0, state_high, next_high)
    other_low = jnp.where(core == 0, next_low, state_low)
    other_high = jnp.where(core == 0, next_high, state_high)
    for which, (cs, at_low, at_high, rows, out) in enumerate(
        (
            (c[...], own_low, own_high, rows_mine, own),
            (received[:, 768:], other_low, other_high, rows_theirs, other),
        )
    ):
        carried = dot(cs[:, :128], at_low, NT) + dot(cs[:, 128:], at_high, NT)
        cols = jnp.exp(columns_of(rows))
        for pair in range(HALF // 2):
            lanes = slice(pair * 128, (pair + 1) * 128)
            out[:, lanes] = (inside[which, :, lanes] + spread(cols, 2 * pair) * carried[:, lanes]).astype(BF16)


SCALE = HEAD_SIZE ** (-0.5)
SCALE2 = SCALE * math.log2(math.e)
KEYS = 2 * BLOCK


def attend_kernel(place, q0, q1, q2, q3, kv_own, kv_other, partial0, partial1, partial2, partial3, acc, top, total):
    row, col, core = place[0], place[1], place[2]
    queries = (q0, q1, q2, q3)
    partials = (partial0, partial1, partial2, partial3)

    def pieces(at):
        both = jnp.concatenate([kv_own[at], kv_other[at]], axis=0)
        return both[:, :HEAD_SIZE], both[:, HEAD_SIZE:]

    def stacked(k):
        return jnp.concatenate([queries[k][:, h * 128 : (h + 1) * 128] for h in range(4)], axis=0)

    keys, values = pieces(row)
    sub = lax.broadcasted_iota(jnp.int32, (KEYS, 512), 0)
    lane = lax.broadcasted_iota(jnp.int32, (KEYS, 512), 1)
    chip = row * NX + col
    key_place = jnp.where(
        sub < BLOCK, (chip * 2 + core) * BLOCK + sub, (chip * 2 + 1 - core) * BLOCK + sub - BLOCK
    )
    for k in range(4):
        query_chip = row * NX + lax.rem(col + k, NX)
        query_place = (query_chip * 2 + core) * BLOCK + lax.rem(lane, BLOCK)
        visible = key_place <= query_place
        scores = jnp.where(visible, dot(keys, stacked(k), NT), LOW)
        highest = jnp.max(scores, axis=0, keepdims=True)
        weights = jnp.where(visible, jnp.exp2((scores - highest) * SCALE2), 0.0)
        top[k] = highest
        total[k] = jnp.sum(weights, axis=0, keepdims=True)
        acc[k] = dot(values, weights.astype(BF16), TN)

    def visit(at, _):
        keys, values = pieces(at)
        for k in range(4):
            scores = dot(keys, stacked(k), NT)
            before = top[k]
            highest = jnp.maximum(before, jnp.max(scores, axis=0, keepdims=True))
            weights = jnp.exp2((scores - highest) * SCALE2)
            factor = jnp.exp2((before - highest) * SCALE2)
            top[k] = highest
            total[k] = total[k] * factor + jnp.sum(weights, axis=0, keepdims=True)
            acc[k] = acc[k] * factor + dot(values, weights.astype(BF16), TN)
        return 0

    lax.fori_loop(0, row, visit, 0)
    for k in range(4):
        amount = total[k]
        mean = acc[k] / jnp.maximum(amount, 1e-30)
        for h in range(4):
            lanes = slice(h * 128, (h + 1) * 128)
            partials[k][0:128, lanes] = mean[:, lanes].T.astype(BF16)
        pieces_of = split3(top[k] * SCALE) + split3(amount)
        tag = lax.broadcasted_iota(jnp.int32, (16, 512), 0)
        tail = jnp.zeros((16, 512), F32)
        for i, piece in enumerate(pieces_of):
            tail = jnp.where(tag == i, piece.astype(F32), tail)
        partials[k][128:144, :] = tail.astype(BF16)


def merge_kernel(a, b, c, d, out):
    parts = (a, b, c, d)
    tops, amounts = [], []
    for part in parts:
        tail = part[128:144, :].astype(F32)
        tops.append(tail[0:1] + tail[1:2] + tail[2:3])
        amounts.append(tail[3:4] + tail[4:5] + tail[5:6])
    highest = functools.reduce(jnp.maximum, tops)
    weights = [amount * jnp.exp(t - highest) for t, amount in zip(tops, amounts)]
    whole = sum(weights)
    rows = jnp.concatenate([w / whole for w in weights] + [jnp.zeros((4, 512), F32)], axis=0)
    for h in range(4):
        lanes = slice(h * 128, (h + 1) * 128)
        cols = columns_of(rows[:, lanes])
        result = sum(cols[:, i : i + 1] * part[0:128, lanes].astype(F32) for i, part in enumerate(parts))
        out[:, lanes] = result.astype(BF16)


def shift(array, axis, size, by):
    return lax.ppermute(array, axis, [(i, (i + by) % size) for i in range(size)])


def swap(array, axis, size, mask):
    return lax.ppermute(array, axis, [(i, i ^ mask) for i in range(size)])


def on_device(
    mamba_input,
    step,
    log_decay,
    state_in,
    state_out,
    skip_gain,
    queries,
    keys,
    values,
    residual,
    norm_gain,
):
    core = lax.axis_index("c")
    place = jnp.stack([lax.axis_index("y"), lax.axis_index("x"), core]).astype(jnp.int32)
    b_in = state_in.reshape(BLOCK, SDIM)
    c_in = state_out.reshape(BLOCK, SDIM)

    kv = jnp.concatenate([keys, values], axis=1)
    copies = jnp.broadcast_to(kv[None], (NY, BLOCK, 2 * HEAD_SIZE))
    kv_own = lax.all_to_all(copies, "y", 0, 0, tiled=True)
    kv_other = swap(kv_own, "c", NC, 1)

    send, rows_send, rows_own = call(
        prepare_kernel,
        (
            shape((BLOCK, 1024), BF16),
            shape((16, BLOCK), F32),
            shape((16, BLOCK), F32),
        ),
        cost=cost(1),
        inputs=5,
    )(place, mamba_input, step, log_decay, b_in, c_in)
    received = swap(send, "c", NC, 1)
    rows_other = swap(rows_send, "c", NC, 1)
    gains = jnp.repeat(lax.dynamic_slice(skip_gain, (core * HALF,), (HALF,)), MDIM)[None, :]
    payload, first_state, inside = call(
        states_kernel,
        (
            shape((CHIPS, 40, 128), BF16),
            shape((512, SDIM), F32),
            shape((2, BLOCK, 512), F32),
        ),
        cost=cost(3),
        inputs=7,
    )(place, mamba_input, b_in, c_in, rows_own, received, rows_other, gains)

    gathered = [queries] + [shift(queries, "x", NX, -k) for k in range(1, NX)]

    arrived = lax.all_to_all(payload, ("y", "x"), 0, 0, tiled=True)
    partials = call(
        attend_kernel,
        tuple(shape((144, 512), BF16) for _ in range(4)),
        scratch=[pltpu.VMEM((4, 128, 512), F32), pltpu.VMEM((4, 1, 512), F32), pltpu.VMEM((4, 1, 512), F32)],
        cost=cost(8),
        inputs=6,
    )(place, *gathered, kv_own, kv_other)
    entering = call(scan_kernel, shape((CHIPS, 32, 128), BF16), cost=cost(1), scalars=0, inputs=1)(arrived)
    returned = lax.all_to_all(entering, ("y", "x"), 0, 0, tiled=True)
    back = [partials[0]] + [shift(partials[k], "x", NX, k) for k in range(1, NX)]
    attn_out = call(merge_kernel, shape((BLOCK, 512), BF16), cost=cost(1), scalars=0, inputs=4)(*back)

    widened = residual.astype(F32)
    squares = jnp.sum(widened * widened, axis=1)
    for mask in (1, 2, 4):
        squares = squares + swap(squares, "z", NZ, mask)
    normed = (widened * lax.rsqrt(squares / D + 1e-05)[:, None] * norm_gain[None, :]).astype(BF16)

    own, other = call(
        finish_kernel,
        (shape((BLOCK, 512), BF16), shape((BLOCK, 512), BF16)),
        cost=cost(2),
        inputs=7,
    )(place, returned, first_state, inside, c_in, received, rows_own, rows_other)
    theirs = swap(other, "c", NC, 1)
    mamba_out = jnp.where(
        core == 0, jnp.concatenate([own, theirs], axis=1), jnp.concatenate([theirs, own], axis=1)
    )
    return mamba_out, attn_out, normed


def solution(mesh):
    grid = Mesh(mesh.devices.reshape(NY, NX, NC, NZ), ("y", "x", "c", "z"))
    ctx = ("y", "x", "c")
    placed = (
        P(ctx, "z"),
        P(ctx, "z"),
        P(ctx, "z"),
        P(ctx, "z", None),
        P(ctx, "z", None),
        P("z"),
        P(ctx, "z"),
        P(ctx, "z"),
        P(ctx, "z"),
        P(ctx, "z"),
        P("z"),
    )
    return jax.shard_map(
        on_device,
        mesh=grid,
        in_specs=placed,
        out_specs=(P(ctx, "z"), P(ctx, "z"), P(ctx, "z")),
        check_vma=False,
    )
```

```python
import functools
import math

import jax
import jax.numpy as jnp
from jax import lax
from jax.experimental import pallas as pl
from jax.experimental.pallas import tpu as pltpu
from jax.sharding import Mesh, PartitionSpec as P

D = 8192
MDIM = 64
SDIM = 256
BLOCK = 128
HEAD_SIZE = 128
NY, NX, NC, NZ = 8, 4, 2, 8
CHIPS = NY * NX
HALF = 8
LOW = -1e30
F32 = jnp.float32
BF16 = jnp.bfloat16
NT = (((1,), (1,)), ((), ()))
TN = (((0,), (0,)), ((), ()))
VMEM = pl.BlockSpec(memory_space=pltpu.VMEM)
SMEM = pl.BlockSpec(memory_space=pltpu.SMEM)


def dot(a, b, dims=(((1,), (0,)), ((), ())), precision=None):
    return lax.dot_general(a, b, dims, preferred_element_type=F32, precision=precision)


def call(kernel, outs, scratch=(), cost=None, scalars=1, inputs=1, after=0):
    given = scalars + inputs

    def body(*refs):
        kernel(*refs[:given], *refs[given + after :])

    return pl.pallas_call(
        body,
        out_shape=outs,
        in_specs=[SMEM] * scalars + [VMEM] * inputs + [pl.BlockSpec(memory_space=pl.ANY)] * after,
        out_specs=jax.tree.map(lambda _: VMEM, outs),
        scratch_shapes=list(scratch),
        compiler_params=pltpu.CompilerParams(vmem_limit_bytes=40 * 1024 * 1024),
        cost_estimate=cost,
    )


def shape(dims, dtype):
    return jax.ShapeDtypeStruct(dims, dtype)


def cost(us):
    return pl.CostEstimate(flops=int(us * 1e6 * 1000), bytes_accessed=int(us * 3e6), transcendentals=0)


def split3(v):
    hi = v.astype(BF16)
    rest = v - hi.astype(F32)
    mid = rest.astype(BF16)
    lo = (rest - mid.astype(F32)).astype(BF16)
    return hi, mid, lo


def prepare_kernel(place, x, step, decay, b, c, q, send, rows_keep):
    core = place[2]
    tri = (
        lax.broadcasted_iota(jnp.int32, (BLOCK, BLOCK), 0)
        <= lax.broadcasted_iota(jnp.int32, (BLOCK, BLOCK), 1)
    ).astype(F32)
    eye = (
        lax.broadcasted_iota(jnp.int32, (BLOCK, BLOCK), 0)
        == lax.broadcasted_iota(jnp.int32, (BLOCK, BLOCK), 1)
    ).astype(F32)
    run = dot(decay[...], tri, TN, lax.Precision.HIGHEST)
    steps = dot(step[...], eye, TN, lax.Precision.HIGHEST)
    low = jnp.concatenate([run[:HALF], steps[:HALF]], axis=0)
    high = jnp.concatenate([run[HALF:], steps[HALF:]], axis=0)
    rows_keep[...] = jnp.where(core == 0, low, high)
    send[0:BLOCK, :512] = jnp.where(core == 0, x[:, 512:], x[:, :512])
    send[0:BLOCK, 512:768] = b[...]
    send[0:BLOCK, 768:1024] = c[...]
    send[0:BLOCK, 1024:] = q[...]
    send[BLOCK:, 384:] = jnp.zeros((16, 1152), BF16)
    for i, piece in enumerate(split3(jnp.where(core == 0, high, low))):
        send[BLOCK:, i * 128 : (i + 1) * 128] = piece


def received_rows(received):
    tail = received[BLOCK:, 0:384].astype(F32)
    return tail[:, 0:128] + tail[:, 128:256] + tail[:, 256:384]


def columns_of(rows):
    padded = jnp.concatenate([rows, jnp.zeros((BLOCK - rows.shape[0], BLOCK), F32)], axis=0)
    return padded.T


def spread(cols, first):
    lane = lax.broadcasted_iota(jnp.int32, (BLOCK, 128), 1)
    return jnp.where(lane < MDIM, cols[:, first : first + 1], cols[:, first + 1 : first + 2])


def states_kernel(place, x, b, c, rows_own, received, gain, payload, first_state, inside):
    core = place[2]
    causal = lax.broadcasted_iota(jnp.int32, (BLOCK, BLOCK), 0) >= lax.broadcasted_iota(
        jnp.int32, (BLOCK, BLOCK), 1
    )
    x_own = jnp.where(core == 0, x[:, :512], x[:, 512:])
    blocks = (
        (x_own, b[...], c[...], rows_own[...]),
        (
            received[0:BLOCK, :512],
            received[0:BLOCK, 512:768],
            received[0:BLOCK, 768:1024],
            received_rows(received),
        ),
    )
    gains = gain[...]
    states = []
    totals = []
    for which, (xs, bs, cs, rows) in enumerate(blocks):
        cols = columns_of(rows)
        mixed = dot(cs, bs, NT)
        ends = rows[:, BLOCK - 1 : BLOCK]
        totals.append(ends)
        scaled = []
        for pair in range(HALF // 2):
            parts = []
            for head in (2 * pair, 2 * pair + 1):
                gap = cols[:, head : head + 1] - rows[head : head + 1, :]
                grown = jnp.exp(jnp.where(causal, gap, LOW))
                weight = (grown * mixed * rows[HALF + head : HALF + head + 1, :]).astype(BF16)
                parts.append(dot(weight, xs[:, head * MDIM : (head + 1) * MDIM]))
            lanes = slice(pair * 128, (pair + 1) * 128)
            wide = xs[:, lanes].astype(F32)
            inside[which, :, lanes] = jnp.concatenate(parts, axis=1) + gains[:, lanes] * wide
            lane = lax.broadcasted_iota(jnp.int32, (1, 128), 1)
            end = jnp.where(lane < MDIM, ends[2 * pair : 2 * pair + 1], ends[2 * pair + 1 : 2 * pair + 2])
            to_end = jnp.exp(end - spread(cols, 2 * pair)) * spread(cols, HALF + 2 * pair)
            scaled.append((to_end * wide).astype(BF16))
        states.append(dot(jnp.concatenate(scaled, axis=1), bs, TN))
    lengths = totals[0] + totals[1]
    for head in range(HALF):
        rows = slice(head * MDIM, (head + 1) * MDIM)
        own, other = states[0][rows], states[1][rows]
        gain_own = jnp.exp(totals[0][head : head + 1])
        gain_other = jnp.exp(totals[1][head : head + 1])
        first_state[rows, :] = jnp.where(core == 0, own, other)
        joint = jnp.where(core == 0, gain_other * own + other, gain_own * other + own).astype(BF16)
        hi, mid, lo = split3(jnp.broadcast_to(lengths[head : head + 1], (8, 128)))
        tag = lax.broadcasted_iota(jnp.int32, (8, 128), 0)
        total = jnp.where(tag == 0, hi.astype(F32), jnp.where(tag == 1, mid.astype(F32), lo.astype(F32)))
        for part in range(4):
            chunk = head * 4 + part
            payload[chunk, 0:16, :] = joint[part * 16 : (part + 1) * 16, :128]
            payload[chunk, 16:32, :] = joint[part * 16 : (part + 1) * 16, 128:]
            payload[chunk, 32:40, :] = total.astype(BF16)


def scan_kernel(arrived, entering):
    state = jnp.zeros((32, 128), F32)
    for chip in range(CHIPS):
        entering[chip] = state.astype(BF16)
        tail = arrived[chip, 32:40, :].astype(F32)
        gain = jnp.exp(tail[0:1] + tail[1:2] + tail[2:3])
        state = gain * state + arrived[chip, 0:32, :].astype(F32)


def finish_kernel(place, entering, first_state, inside, c, received, rows_own, part_other, own, other):
    core = place[2]
    other[BLOCK:, :] = part_other[...]
    state_low = entering[:, 0:16, :].reshape(512, 128)
    state_high = entering[:, 16:32, :].reshape(512, 128)
    rows_mine, rows_theirs = rows_own[...], received_rows(received)
    first_total = jnp.where(core == 0, rows_mine[:HALF], rows_theirs[:HALF])[:, BLOCK - 1 : BLOCK]
    gain = jnp.exp(first_total)
    low, high = [], []
    for head in range(HALF):
        rows = slice(head * MDIM, (head + 1) * MDIM)
        low.append(gain[head : head + 1] * state_low[rows].astype(F32) + first_state[rows, :128])
        high.append(gain[head : head + 1] * state_high[rows].astype(F32) + first_state[rows, 128:])
    next_low = jnp.concatenate(low, axis=0).astype(BF16)
    next_high = jnp.concatenate(high, axis=0).astype(BF16)
    own_low = jnp.where(core == 0, state_low, next_low)
    own_high = jnp.where(core == 0, state_high, next_high)
    other_low = jnp.where(core == 0, next_low, state_low)
    other_high = jnp.where(core == 0, next_high, state_high)
    for which, (cs, at_low, at_high, rows, out) in enumerate(
        (
            (c[...], own_low, own_high, rows_mine, own),
            (received[0:BLOCK, 768:1024], other_low, other_high, rows_theirs, other),
        )
    ):
        carried = dot(cs[:, :128], at_low, NT) + dot(cs[:, 128:], at_high, NT)
        cols = jnp.exp(columns_of(rows))
        for pair in range(HALF // 2):
            lanes = slice(pair * 128, (pair + 1) * 128)
            out[0:BLOCK, lanes] = (inside[which, :, lanes] + spread(cols, 2 * pair) * carried[:, lanes]).astype(BF16)


SCALE = HEAD_SIZE ** (-0.5)
SCALE2 = SCALE * math.log2(math.e)
ROWS = 2 * 4 * BLOCK
PIECE = 512


def attend_kernel(first, last, columns, place, q_own, received, *refs):
    row, col, core = place[0], place[1], place[2]
    kvs, refs = refs[:columns], refs[columns:]
    if not first:
        before, refs = refs[:2], refs[2:]
    outs, (q_all, acc, top, total) = refs[:2], refs[2:]
    for block, (source, start) in enumerate(((q_own, 0), (received, 1024))):
        for h in range(4):
            at = (block * 4 + h) * BLOCK
            q_all[at : at + BLOCK, :] = source[0:BLOCK, start + h * 128 : start + (h + 1) * 128]

    def absorb(keys, values, start, visible=None):
        lanes = slice(start, start + PIECE)
        scores = dot(keys, q_all[lanes, :], NT)
        if visible is not None:
            scores = jnp.where(visible, scores, 2 * LOW)
        old = top[:, lanes]
        highest = jnp.maximum(old, jnp.max(scores, axis=0, keepdims=True))
        weights = jnp.exp2((scores - highest) * SCALE2)
        factor = jnp.exp2((old - highest) * SCALE2)
        top[:, lanes] = highest
        total[:, lanes] = total[:, lanes] * factor + jnp.sum(weights, axis=0, keepdims=True)
        acc[:, lanes] = acc[:, lanes] * factor + dot(values, weights.astype(BF16), TN)

    def tile(kv, at, count):
        both = kv[pl.ds(at, count)].reshape(count * BLOCK, 2 * HEAD_SIZE)
        return both[:, :HEAD_SIZE], both[:, HEAD_SIZE:]

    def whole_rows(kv, number):
        def visit(pair, carry):
            keys, values = tile(kv, 2 * pair, 2)
            for start in range(0, ROWS, PIECE):
                absorb(keys, values, start)
            return carry

        lax.fori_loop(0, number // 2, visit, 0)

        @pl.when(lax.rem(number, 2) == 1)
        def _():
            keys, values = tile(kv, number - 1, 1)
            for start in range(0, ROWS, PIECE):
                absorb(keys, values, start)

    if first:
        top[...] = jnp.full((1, ROWS), LOW, F32)
        total[...] = jnp.zeros((1, ROWS), F32)
        acc[...] = jnp.zeros((BLOCK, ROWS), F32)
        keys, values = tile(kvs[0], row, 1)
        sub = lax.broadcasted_iota(jnp.int32, (BLOCK, PIECE), 0)
        lane = lax.rem(lax.broadcasted_iota(jnp.int32, (BLOCK, PIECE), 1), BLOCK)
        for block in range(2):
            query_core = core if block == 0 else 1 - core
            visible = core * BLOCK + sub <= query_core * BLOCK + lane
            absorb(keys, values, block * PIECE, visible)
        whole_rows(kvs[0], row)
    else:
        acc[...] = before[0][...]
        top[...] = before[1][0:1]
        total[...] = before[1][1:2]
        if last:
            number = row + (lax.rem(col + 2, NX) < col).astype(jnp.int32)
            whole_rows(kvs[0], jnp.minimum(number, 4))
            whole_rows(kvs[1], jnp.maximum(number - 4, 0))
        else:
            whole_rows(kvs[0], row + (lax.rem(col + 3, NX) < col).astype(jnp.int32))
            whole_rows(kvs[1], row + (lax.rem(col + 1, NX) < col).astype(jnp.int32))
    if not last:
        outs[0][...] = acc[...]
        outs[1][0:1] = top[...]
        outs[1][1:2] = total[...]
        return
    tag = lax.broadcasted_iota(jnp.int32, (16, 512), 0)
    for block in range(2):
        lanes = slice(block * 512, (block + 1) * 512)
        amount = total[:, lanes]
        mean = acc[:, lanes] / jnp.maximum(amount, 1e-30)
        for h in range(4):
            part = slice(h * 128, (h + 1) * 128)
            outs[block][0:BLOCK, part] = mean[:, part].T.astype(BF16)
        tail = jnp.zeros((16, 512), F32)
        for i, piece in enumerate(split3(top[:, lanes] * SCALE) + split3(amount)):
            tail = jnp.where(tag == i, piece.astype(F32), tail)
        outs[block][BLOCK:, :] = tail.astype(BF16)


def attend(first, last, place, q_own, received, kvs, before=(), after=(), us=3):
    if last:
        outs = (shape((BLOCK + 16, 512), BF16),) * 2
    else:
        outs = (shape((BLOCK, ROWS), F32), shape((2, ROWS), F32))
    return call(
        functools.partial(attend_kernel, first, last, len(kvs)),
        outs,
        scratch=[
            pltpu.VMEM((ROWS, HEAD_SIZE), BF16),
            pltpu.VMEM((BLOCK, ROWS), F32),
            pltpu.VMEM((1, ROWS), F32),
            pltpu.VMEM((1, ROWS), F32),
        ],
        cost=cost(us),
        inputs=2 + len(kvs) + len(before),
        after=len(after),
    )(place, q_own, received, *kvs, *before, *after)


def merge_kernel(place, part_own, own, received, mamba_out, attn_out):
    core = place[2]
    mine, theirs = own[...], received[0:BLOCK, :]
    mamba_out[:, :512] = jnp.where(core == 0, mine, theirs)
    mamba_out[:, 512:] = jnp.where(core == 0, theirs, mine)
    tops, amounts = [], []
    for tail in (part_own[BLOCK:, :], received[2 * BLOCK :, :]):
        tail = tail.astype(F32)
        tops.append(tail[0:1] + tail[1:2] + tail[2:3])
        amounts.append(tail[3:4] + tail[4:5] + tail[5:6])
    highest = jnp.maximum(*tops)
    weights = [amount * jnp.exp(t - highest) for t, amount in zip(tops, amounts)]
    whole = weights[0] + weights[1]
    rows = jnp.concatenate([w / whole for w in weights] + [jnp.zeros((6, 512), F32)], axis=0)
    for h in range(4):
        lanes = slice(h * 128, (h + 1) * 128)
        cols = columns_of(rows[:, lanes])
        result = cols[:, 0:1] * part_own[0:BLOCK, lanes].astype(F32)
        result = result + cols[:, 1:2] * received[BLOCK : 2 * BLOCK, lanes].astype(F32)
        attn_out[:, lanes] = result.astype(BF16)


def shift(array, axis, size, by):
    return lax.ppermute(array, axis, [(i, (i + by) % size) for i in range(size)])


def swap(array, axis, size, mask):
    return lax.ppermute(array, axis, [(i, i ^ mask) for i in range(size)])


def on_device(
    mamba_input,
    step,
    log_decay,
    state_in,
    state_out,
    skip_gain,
    queries,
    keys,
    values,
    residual,
    norm_gain,
):
    core = lax.axis_index("c")
    place = jnp.stack([lax.axis_index("y"), lax.axis_index("x"), core]).astype(jnp.int32)
    b_in = state_in.reshape(BLOCK, SDIM)
    c_in = state_out.reshape(BLOCK, SDIM)

    kv = jnp.concatenate([keys, values], axis=1)
    copies = jnp.broadcast_to(kv[None], (NY, BLOCK, 2 * HEAD_SIZE))
    kv_here = lax.all_to_all(copies, "y", 0, 0, tiled=True)

    send, rows_own = call(
        prepare_kernel,
        (shape((BLOCK + 16, 1536), BF16), shape((16, BLOCK), F32)),
        cost=cost(1),
        inputs=6,
        after=1,
    )(place, mamba_input, step, log_decay, b_in, c_in, queries, copies)
    received = swap(send, "c", NC, 1)

    widened = residual.astype(F32)
    squares = jnp.sum(widened * widened, axis=1)
    squares = squares + swap(squares, "z", NZ, 1)
    squares = squares + swap(squares, "z", NZ, 2)

    gains = jnp.repeat(lax.dynamic_slice(skip_gain, (core * HALF,), (HALF,)), MDIM)[None, :]
    payload, first_state, inside = call(
        states_kernel,
        (
            shape((CHIPS, 40, 128), BF16),
            shape((512, SDIM), F32),
            shape((2, BLOCK, 512), F32),
        ),
        cost=cost(3),
        inputs=6,
        after=1,
    )(place, mamba_input, b_in, c_in, rows_own, received, gains, squares)
    arrived = lax.all_to_all(payload, ("y", "x"), 0, 0, tiled=True)

    kv_left = shift(kv_here, "x", NX, 1)
    kv_right = shift(kv_here, "x", NX, -1)
    status = attend(True, False, place, queries, received, [kv_here])

    entering = call(
        scan_kernel, shape((CHIPS, 32, 128), BF16), cost=cost(1), scalars=0, inputs=1, after=3
    )(arrived, kv_left, kv_right, status[1])
    returned = lax.all_to_all(entering, ("y", "x"), 0, 0, tiled=True)

    far_low = shift(kv_left[:4], "x", NX, 1)
    far_high = shift(kv_right[4:], "x", NX, -1)
    squares = squares + swap(squares, "z", NZ, 4)
    normed = (widened * lax.rsqrt(squares / D + 1e-05)[:, None] * norm_gain[None, :]).astype(BF16)
    status = attend(False, False, place, queries, received, [kv_left, kv_right], before=status)
    part_own, part_other = attend(False, True, place, queries, received, [far_low, far_high], before=status)

    own, other = call(
        finish_kernel,
        (shape((BLOCK, 512), BF16), shape((2 * BLOCK + 16, 512), BF16)),
        cost=cost(2),
        inputs=7,
    )(place, returned, first_state, inside, c_in, received, rows_own, part_other)
    theirs = swap(other, "c", NC, 1)
    mamba_out, attn_out = call(
        merge_kernel,
        (shape((BLOCK, 1024), BF16), shape((BLOCK, 512), BF16)),
        cost=cost(2),
        inputs=3,
    )(place, part_own, own, theirs)
    return mamba_out, attn_out, normed


def solution(mesh):
    grid = Mesh(mesh.devices.reshape(NY, NX, NC, NZ), ("y", "x", "c", "z"))
    ctx = ("y", "x", "c")
    placed = (
        P(ctx, "z"),
        P(ctx, "z"),
        P(ctx, "z"),
        P(ctx, "z", None),
        P(ctx, "z", None),
        P("z"),
        P(ctx, "z"),
        P(ctx, "z"),
        P(ctx, "z"),
        P(ctx, "z"),
        P("z"),
    )
    return jax.shard_map(
        on_device,
        mesh=grid,
        in_specs=placed,
        out_specs=(P(ctx, "z"), P(ctx, "z"), P(ctx, "z")),
        check_vma=False,
    )
```

```python
import functools
import math

import jax
import jax.numpy as jnp
from jax import lax
from jax.experimental import pallas as pl
from jax.experimental.pallas import tpu as pltpu
from jax.sharding import Mesh, PartitionSpec as P

D = 8192
MDIM = 64
SDIM = 256
BLOCK = 128
HEAD_SIZE = 128
NY, NX, NC, NZ = 8, 4, 2, 8
CHIPS = NY * NX
HALF = 8
LOW = -1e30
F32 = jnp.float32
BF16 = jnp.bfloat16
NT = (((1,), (1,)), ((), ()))
TN = (((0,), (0,)), ((), ()))
VMEM = pl.BlockSpec(memory_space=pltpu.VMEM)
SMEM = pl.BlockSpec(memory_space=pltpu.SMEM)


def dot(a, b, dims=(((1,), (0,)), ((), ())), precision=None):
    return lax.dot_general(a, b, dims, preferred_element_type=F32, precision=precision)


def call(kernel, outs, scratch=(), cost=None, scalars=1, inputs=1, away=0, after=0):
    given = scalars + inputs + away

    def body(*refs):
        kernel(*refs[:given], *refs[given + after :])

    return pl.pallas_call(
        body,
        out_shape=outs,
        in_specs=[SMEM] * scalars + [VMEM] * inputs + [pl.BlockSpec(memory_space=pl.ANY)] * (away + after),
        out_specs=jax.tree.map(lambda _: VMEM, outs),
        scratch_shapes=list(scratch),
        compiler_params=pltpu.CompilerParams(vmem_limit_bytes=40 * 1024 * 1024),
        cost_estimate=cost,
    )


def shape(dims, dtype):
    return jax.ShapeDtypeStruct(dims, dtype)


def cost(us):
    return pl.CostEstimate(flops=int(us * 1e9), bytes_accessed=int(us * 3e6), transcendentals=0)


def split3(v):
    hi = v.astype(BF16)
    rest = v - hi.astype(F32)
    mid = rest.astype(BF16)
    lo = (rest - mid.astype(F32)).astype(BF16)
    return hi, mid, lo


def prepare_kernel(place, x, step, decay, b, c, q, send, rows_keep):
    core = place[2]
    tri = (
        lax.broadcasted_iota(jnp.int32, (BLOCK, BLOCK), 0)
        <= lax.broadcasted_iota(jnp.int32, (BLOCK, BLOCK), 1)
    ).astype(F32)
    eye = (
        lax.broadcasted_iota(jnp.int32, (BLOCK, BLOCK), 0)
        == lax.broadcasted_iota(jnp.int32, (BLOCK, BLOCK), 1)
    ).astype(F32)
    run = dot(decay[...], tri, TN, lax.Precision.HIGHEST)
    steps = dot(step[...], eye, TN, lax.Precision.HIGHEST)
    low = jnp.concatenate([run[:HALF], steps[:HALF]], axis=0)
    high = jnp.concatenate([run[HALF:], steps[HALF:]], axis=0)
    rows_keep[...] = jnp.where(core == 0, low, high)
    send[0:BLOCK, :512] = jnp.where(core == 0, x[:, 512:], x[:, :512])
    send[0:BLOCK, 512:768] = b[...]
    send[0:BLOCK, 768:1024] = c[...]
    send[0:BLOCK, 1024:] = q[...]
    send[BLOCK:, 384:] = jnp.zeros((16, 1152), BF16)
    for i, piece in enumerate(split3(jnp.where(core == 0, high, low))):
        send[BLOCK:, i * 128 : (i + 1) * 128] = piece


def received_rows(received):
    tail = received[BLOCK:, 0:384].astype(F32)
    return tail[:, 0:128] + tail[:, 128:256] + tail[:, 256:384]


def columns_of(rows):
    padded = jnp.concatenate([rows, jnp.zeros((BLOCK - rows.shape[0], BLOCK), F32)], axis=0)
    return padded.T


def spread(cols, first):
    lane = lax.broadcasted_iota(jnp.int32, (BLOCK, 128), 1)
    return jnp.where(lane < MDIM, cols[:, first : first + 1], cols[:, first + 1 : first + 2])


def first_place(head):
    row, lane = 2 * BLOCK + head % 4 * MDIM, head // 4 * SDIM
    return (slice(row, row + MDIM), slice(lane, lane + SDIM))


def states_kernel(
    place, x, b, c, rows_own, received, gain, q, sums, payload, kept, q_pair, sums_out
):
    core = place[2]
    sums_out[...] = sums[...]
    q_pair[:, :512] = q[...]
    q_pair[:, 512:] = received[0:BLOCK, 1024:]
    causal = lax.broadcasted_iota(jnp.int32, (BLOCK, BLOCK), 0) >= lax.broadcasted_iota(
        jnp.int32, (BLOCK, BLOCK), 1
    )
    x_own = jnp.where(core == 0, x[:, :512], x[:, 512:])
    blocks = (
        (x_own, b[...], c[...], rows_own[...]),
        (
            received[0:BLOCK, :512],
            received[0:BLOCK, 512:768],
            received[0:BLOCK, 768:1024],
            received_rows(received),
        ),
    )
    gains = gain[...]
    states = []
    totals = []
    for which, (xs, bs, cs, rows) in enumerate(blocks):
        cols = columns_of(rows)
        mixed = dot(cs, bs, NT)
        ends = rows[:, BLOCK - 1 : BLOCK]
        totals.append(ends)
        scaled = []
        for pair in range(HALF // 2):
            parts = []
            for head in (2 * pair, 2 * pair + 1):
                gap = cols[:, head : head + 1] - rows[head : head + 1, :]
                grown = jnp.exp(jnp.where(causal, gap, LOW))
                weight = (grown * mixed * rows[HALF + head : HALF + head + 1, :]).astype(BF16)
                parts.append(dot(weight, xs[:, head * MDIM : (head + 1) * MDIM]))
            lanes = slice(pair * 128, (pair + 1) * 128)
            wide = xs[:, lanes].astype(F32)
            inside = jnp.concatenate(parts, axis=1) + gains[:, lanes] * wide
            kept[which * BLOCK : (which + 1) * BLOCK, lanes] = inside.astype(BF16)
            lane = lax.broadcasted_iota(jnp.int32, (1, 128), 1)
            end = jnp.where(lane < MDIM, ends[2 * pair : 2 * pair + 1], ends[2 * pair + 1 : 2 * pair + 2])
            to_end = jnp.exp(end - spread(cols, 2 * pair)) * spread(cols, HALF + 2 * pair)
            scaled.append((to_end * wide).astype(BF16))
        states.append(dot(jnp.concatenate(scaled, axis=1), bs, TN))
    lengths = totals[0] + totals[1]
    for head in range(HALF):
        rows = slice(head * MDIM, (head + 1) * MDIM)
        own, other = states[0][rows], states[1][rows]
        gain_own = jnp.exp(totals[0][head : head + 1])
        gain_other = jnp.exp(totals[1][head : head + 1])
        kept[first_place(head)] = jnp.where(core == 0, own, other).astype(BF16)
        joint = jnp.where(core == 0, gain_other * own + other, gain_own * other + own).astype(BF16)
        hi, mid, lo = split3(jnp.broadcast_to(lengths[head : head + 1], (8, 128)))
        tag = lax.broadcasted_iota(jnp.int32, (8, 128), 0)
        total = jnp.where(tag == 0, hi.astype(F32), jnp.where(tag == 1, mid.astype(F32), lo.astype(F32)))
        for part in range(4):
            chunk = head * 4 + part
            payload[chunk, 0:16, :] = joint[part * 16 : (part + 1) * 16, :128]
            payload[chunk, 16:32, :] = joint[part * 16 : (part + 1) * 16, 128:]
            payload[chunk, 32:40, :] = total.astype(BF16)


def scan_kernel(arrived, sums, after, entering, sums_out):
    sums_out[...] = sums[...]
    state = jnp.zeros((32, 128), F32)
    for chip in range(CHIPS):
        entering[chip] = state.astype(BF16)
        tail = arrived[chip, 32:40, :].astype(F32)
        gain = jnp.exp(tail[0:1] + tail[1:2] + tail[2:3])
        state = gain * state + arrived[chip, 0:32, :].astype(F32)


def finish_kernel(place, entering, c, received, rows_own, sums, kept, parts, own, other, sums_out):
    core = place[2]
    sums_out[...] = sums[...]
    other[:, 512:] = parts[:, WIDE:]
    state_low = entering[:, 0:16, :].reshape(512, 128)
    state_high = entering[:, 16:32, :].reshape(512, 128)
    rows_mine, rows_theirs = rows_own[...], received_rows(received)
    first_total = jnp.where(core == 0, rows_mine[:HALF], rows_theirs[:HALF])[:, BLOCK - 1 : BLOCK]
    gain = jnp.exp(first_total)
    low, high = [], []
    for head in range(HALF):
        rows = slice(head * MDIM, (head + 1) * MDIM)
        first = kept[first_place(head)].astype(F32)
        low.append(gain[head : head + 1] * state_low[rows].astype(F32) + first[:, :128])
        high.append(gain[head : head + 1] * state_high[rows].astype(F32) + first[:, 128:])
    next_low = jnp.concatenate(low, axis=0).astype(BF16)
    next_high = jnp.concatenate(high, axis=0).astype(BF16)
    own_low = jnp.where(core == 0, state_low, next_low)
    own_high = jnp.where(core == 0, state_high, next_high)
    other_low = jnp.where(core == 0, next_low, state_low)
    other_high = jnp.where(core == 0, next_high, state_high)
    for which, (cs, at_low, at_high, rows, out) in enumerate(
        (
            (c[...], own_low, own_high, rows_mine, own),
            (received[0:BLOCK, 768:1024], other_low, other_high, rows_theirs, other),
        )
    ):
        carried = dot(cs[:, :128], at_low, NT) + dot(cs[:, 128:], at_high, NT)
        cols = jnp.exp(columns_of(rows))
        for pair in range(HALF // 2):
            lanes = slice(pair * 128, (pair + 1) * 128)
            out[:, lanes] = (
                kept[which * BLOCK : (which + 1) * BLOCK, lanes].astype(F32)
                + spread(cols, 2 * pair) * carried[:, lanes]
            ).astype(BF16)


SCALE = HEAD_SIZE ** (-0.5)
SCALE2 = SCALE * math.log2(math.e)
ROWS = 2 * 4 * BLOCK
TAIL = 128


def copies_kernel(keys, values, out, both, done):
    into = [
        pltpu.make_async_copy(keys, both.at[:, pl.ds(0, HEAD_SIZE)], done.at[0]),
        pltpu.make_async_copy(values, both.at[:, pl.ds(HEAD_SIZE, HEAD_SIZE)], done.at[1]),
    ]
    for copy in into:
        copy.start()
    for copy in into:
        copy.wait()
    away = [pltpu.make_async_copy(both, out.at[i], done.at[2 + i]) for i in range(NY)]
    for copy in away:
        copy.start()
    for copy in away:
        copy.wait()


WIDE = 512 + TAIL


def marked(tail, h, top, amount):
    lane = lax.broadcasted_iota(jnp.int32, (BLOCK, TAIL), 1)
    for i, piece in enumerate(split3(top) + split3(amount)):
        tail = jnp.where(lane == h * 6 + i, piece.astype(F32), tail)
    return tail


def part_of(ref, start, h):
    t = ref[:, start + 512 : start + WIDE].astype(F32)
    at = h * 6
    top = t[:, at : at + 1] + t[:, at + 1 : at + 2] + t[:, at + 2 : at + 3]
    amount = t[:, at + 3 : at + 4] + t[:, at + 4 : at + 5] + t[:, at + 5 : at + 6]
    return ref[:, start + h * 128 : start + (h + 1) * 128].astype(F32), top, amount


def combine(parts):
    highest = functools.reduce(jnp.maximum, [top for _, top, _ in parts])
    weights = [amount * jnp.exp(top - highest) for _, top, amount in parts]
    whole = sum(weights)
    scale = 1.0 / jnp.maximum(whole, 1e-30)
    return sum((w * scale) * mean for w, (mean, _, _) in zip(weights, parts)), highest, whole


def absorb(q, acc, top, kv, count, number, query_core=None, row=None, core=None):
    both = kv[0:count].reshape(count * BLOCK, 2 * HEAD_SIZE)
    keys = both[:, :HEAD_SIZE]
    values = jnp.concatenate([both[:, HEAD_SIZE:], jnp.ones((count * BLOCK, 128), BF16)], axis=1)
    place_of_key = lax.broadcasted_iota(jnp.int32, (1, count * BLOCK), 1)
    hidden = jnp.where(place_of_key < number * BLOCK, 0.0, 2 * LOW)
    for piece in range(ROWS // BLOCK):
        rows = slice(piece * BLOCK, (piece + 1) * BLOCK)
        block, h = piece // 4, piece % 4
        at = block * 512 + h * 128
        scores = dot(q[:, at : at + 128], keys, NT)
        if query_core is not None:
            theirs = query_core[block]
            sub = lax.broadcasted_iota(jnp.int32, (BLOCK, count * BLOCK), 0)
            lane = lax.broadcasted_iota(jnp.int32, (BLOCK, count * BLOCK), 1)
            limit = row * BLOCK + jnp.where(core == theirs, sub, jnp.where(core < theirs, BLOCK - 1, -1))
            scores = jnp.where(lane <= limit, scores, 2 * LOW)
            highest = jnp.maximum(jnp.max(scores, axis=1, keepdims=True), LOW)
            weights = jnp.exp2((scores - highest) * SCALE2).astype(BF16)
            top[rows, :] = jnp.broadcast_to(highest, (BLOCK, 128))
            acc[rows, :] = dot(weights, values)
        else:
            scores = scores + hidden
            old = top[rows, :]
            highest = jnp.maximum(old, jnp.max(scores, axis=1, keepdims=True))
            weights = jnp.exp2((scores - highest[:, 0:1]) * SCALE2).astype(BF16)
            factor = jnp.exp2((old - highest) * SCALE2)
            top[rows, :] = highest
            acc[rows, :] = acc[rows, :] * jnp.concatenate([factor, factor], axis=1) + dot(weights, values)


def near_kernel(place, q, kv, out, marks, token, acc, top):
    row, core = place[0], place[2]
    token[...] = jnp.zeros((1, 128), F32)
    for count, here in ((8, row >= 4), (4, row < 4)):

        @pl.when(here)
        def _():
            absorb(q, acc, top, kv, count, 0, (core, 1 - core), row, core)

    out[...] = acc[:, 0:128]
    lane = lax.broadcasted_iota(jnp.int32, (BLOCK, 128), 1)
    both = jnp.zeros((BLOCK, 128), F32)
    for piece in range(ROWS // BLOCK):
        rows = slice(piece * BLOCK, (piece + 1) * BLOCK)
        both = jnp.where(lane == 2 * piece, top[rows, :], both)
        both = jnp.where(lane == 2 * piece + 1, acc[rows, 128:], both)
    marks[...] = both


def far_kernel(place, q, left, right, far, before, marks, sums, parts, sums_out, acc, top):
    row, col = place[0], place[1]
    sums_out[...] = sums[...]
    for piece in range(ROWS // BLOCK):
        rows = slice(piece * BLOCK, (piece + 1) * BLOCK)
        top[rows, :] = jnp.broadcast_to(marks[:, 2 * piece : 2 * piece + 1], (BLOCK, 128))
        acc[rows, 0:128] = before[rows, :]
        acc[rows, 128:] = jnp.broadcast_to(marks[:, 2 * piece + 1 : 2 * piece + 2], (BLOCK, 128))
    for kv, step in ((left, 3), (right, 1), (far, 2)):
        number = row + (lax.rem(col + step, NX) < col).astype(jnp.int32)
        for count, here in ((8, number > 4), (4, (number > 0) & (number <= 4))):

            @pl.when(here)
            def _():
                absorb(q, acc, top, kv, count, number)

    for block in range(2):
        start = block * WIDE
        tail = jnp.zeros((BLOCK, TAIL), F32)
        for h in range(4):
            rows = slice((block * 4 + h) * BLOCK, (block * 4 + h + 1) * BLOCK)
            amount = acc[rows, 128:]
            mean = acc[rows, 0:128] / jnp.maximum(amount, 1e-30)
            parts[:, start + h * 128 : start + (h + 1) * 128] = mean.astype(BF16)
            tail = marked(tail, h, top[rows, :] * SCALE, amount)
        parts[:, start + 512 : start + WIDE] = tail.astype(BF16)


def merge_kernel(place, parts, own, received, mamba_out, attn_out):
    core = place[2]
    mine, theirs = own[...], received[:, :512]
    mamba_out[:, :512] = jnp.where(core == 0, mine, theirs)
    mamba_out[:, 512:] = jnp.where(core == 0, theirs, mine)
    for h in range(4):
        mean, _, _ = combine([part_of(parts, 0, h), part_of(received, 512, h)])
        attn_out[:, h * 128 : (h + 1) * 128] = mean.astype(BF16)


def shift(array, axis, size, by):
    return lax.ppermute(array, axis, [(i, (i + by) % size) for i in range(size)])


def swap(array, axis, size, mask):
    return lax.ppermute(array, axis, [(i, i ^ mask) for i in range(size)])


def on_device(
    mamba_input,
    step,
    log_decay,
    state_in,
    state_out,
    skip_gain,
    queries,
    keys,
    values,
    residual,
    norm_gain,
):
    core = lax.axis_index("c")
    place = jnp.stack([lax.axis_index("y"), lax.axis_index("x"), core]).astype(jnp.int32)
    b_in = state_in.reshape(BLOCK, SDIM)
    c_in = state_out.reshape(BLOCK, SDIM)

    anywhere = pl.BlockSpec(memory_space=pl.ANY)
    copies = pl.pallas_call(
        copies_kernel,
        out_shape=shape((NY, BLOCK, 2 * HEAD_SIZE), BF16),
        in_specs=[anywhere, anywhere],
        out_specs=anywhere,
        scratch_shapes=[pltpu.VMEM((BLOCK, 2 * HEAD_SIZE), BF16), pltpu.SemaphoreType.DMA((2 + NY,))],
        cost_estimate=cost(1),
    )(keys, values)
    kv_here = lax.all_to_all(copies, "y", 0, 0, tiled=True)

    send, rows_own = call(
        prepare_kernel,
        (shape((BLOCK + 16, 1536), BF16), shape((16, BLOCK), F32)),
        cost=cost(1),
        inputs=6,
        after=1,
    )(place, mamba_input, step, log_decay, b_in, c_in, queries, copies)
    received = swap(send, "c", NC, 1)

    widened = residual.astype(F32)
    sums = jnp.sum(widened * widened, axis=1).reshape(1, BLOCK)
    sums = sums + swap(sums, "z", NZ, 1)

    gains = jnp.repeat(lax.dynamic_slice(skip_gain, (core * HALF,), (HALF,)), MDIM)[None, :]
    payload, kept, q_near, sums = call(
        states_kernel,
        (
            shape((CHIPS, 40, 128), BF16),
            shape((512, 512), BF16),
            shape((BLOCK, 1024), BF16),
            shape((1, BLOCK), F32),
        ),
        cost=cost(3),
        inputs=8,
    )(place, mamba_input, b_in, c_in, rows_own, received, gains, queries, sums)
    arrived = lax.all_to_all(payload, ("y", "x"), 0, 0, tiled=True)

    kv_far = shift(kv_here, "x", NX, 2)
    kv_left = shift(kv_here, "x", NX, 1)
    kv_right = shift(kv_here, "x", NX, -1)
    wide = [pltpu.VMEM((ROWS, 256), F32), pltpu.VMEM((ROWS, 128), F32)]
    near, marks, token = call(
        near_kernel,
        (shape((ROWS, 128), F32), shape((BLOCK, 128), F32), shape((1, 128), F32)),
        scratch=wide,
        cost=cost(0.05),
        inputs=2,
    )(place, q_near, kv_here)

    entering, sums = call(
        scan_kernel,
        (shape((CHIPS, 32, 128), BF16), shape((1, BLOCK), F32)),
        cost=cost(1),
        scalars=0,
        inputs=3,
    )(arrived, sums, token)
    returned = lax.all_to_all(entering, ("y", "x"), 0, 0, tiled=True)

    sums = sums + swap(sums, "z", NZ, 4)
    parts, sums = call(
        far_kernel,
        (shape((BLOCK, 2 * WIDE), BF16), shape((1, BLOCK), F32)),
        scratch=wide,
        cost=cost(0.05),
        inputs=7,
    )(place, q_near, kv_left, kv_right, kv_far, near, marks, sums)
    own, other, sums = call(
        finish_kernel,
        (shape((BLOCK, 512), BF16), shape((BLOCK, 1024 + TAIL), BF16), shape((1, BLOCK), F32)),
        cost=cost(0.05),
        inputs=7,
    )(place, returned, c_in, received, rows_own, sums, kept, parts)
    theirs = swap(other, "c", NC, 1)
    sums = sums + swap(sums, "z", NZ, 2)
    scale = lax.rsqrt(sums.reshape(BLOCK, 1) / D + 1e-05)
    normed = (widened * scale * norm_gain[None, :]).astype(BF16)

    mamba_out, attn_out = call(
        merge_kernel,
        (shape((BLOCK, 1024), BF16), shape((BLOCK, 512), BF16)),
        cost=cost(2),
        inputs=3,
    )(place, parts, own, theirs)
    return mamba_out, attn_out, normed


def solution(mesh):
    grid = Mesh(mesh.devices.reshape(NY, NX, NC, NZ), ("y", "x", "c", "z"))
    ctx = ("y", "x", "c")
    placed = (
        P(ctx, "z"),
        P(ctx, "z"),
        P(ctx, "z"),
        P(ctx, "z", None),
        P(ctx, "z", None),
        P("z"),
        P(ctx, "z"),
        P(ctx, "z"),
        P(ctx, "z"),
        P(ctx, "z"),
        P("z"),
    )
    return jax.shard_map(
        on_device,
        mesh=grid,
        in_specs=placed,
        out_specs=(P(ctx, "z"), P(ctx, "z"), P(ctx, "z")),
        check_vma=False,
    )
```

```python
import functools
import math

import jax
import jax.numpy as jnp
from jax import lax
from jax.experimental import pallas as pl
from jax.experimental.pallas import tpu as pltpu
from jax.sharding import Mesh, PartitionSpec as P

D = 8192
MDIM = 64
SDIM = 256
BLOCK = 128
HEAD_SIZE = 128
NY, NX, NC, NZ = 8, 4, 2, 8
CHIPS = NY * NX
HALF = 8
LOW = -1e30
F32 = jnp.float32
BF16 = jnp.bfloat16
NT = (((1,), (1,)), ((), ()))
TN = (((0,), (0,)), ((), ()))
VMEM = pl.BlockSpec(memory_space=pltpu.VMEM)
SMEM = pl.BlockSpec(memory_space=pltpu.SMEM)


def dot(a, b, dims=(((1,), (0,)), ((), ())), precision=None):
    return lax.dot_general(a, b, dims, preferred_element_type=F32, precision=precision)


def call(kernel, outs, scratch=(), cost=None, scalars=1, inputs=1, away=0, after=0):
    given = scalars + inputs + away

    def body(*refs):
        kernel(*refs[:given], *refs[given + after :])

    return pl.pallas_call(
        body,
        out_shape=outs,
        in_specs=[SMEM] * scalars + [VMEM] * inputs + [pl.BlockSpec(memory_space=pl.ANY)] * (away + after),
        out_specs=jax.tree.map(lambda _: VMEM, outs),
        scratch_shapes=list(scratch),
        compiler_params=pltpu.CompilerParams(vmem_limit_bytes=28 * 1024 * 1024),
        cost_estimate=cost,
    )


def shape(dims, dtype):
    return jax.ShapeDtypeStruct(dims, dtype)


def cost(us):
    return pl.CostEstimate(flops=int(us * 1e9), bytes_accessed=int(us * 3e6), transcendentals=0)


def split3(v):
    hi = v.astype(BF16)
    rest = v - hi.astype(F32)
    mid = rest.astype(BF16)
    lo = (rest - mid.astype(F32)).astype(BF16)
    return hi, mid, lo


def prepare_kernel(place, x, step, decay, b, c, q, send, rows_keep):
    core = place[2]
    tri = (
        lax.broadcasted_iota(jnp.int32, (BLOCK, BLOCK), 0)
        <= lax.broadcasted_iota(jnp.int32, (BLOCK, BLOCK), 1)
    ).astype(F32)
    eye = (
        lax.broadcasted_iota(jnp.int32, (BLOCK, BLOCK), 0)
        == lax.broadcasted_iota(jnp.int32, (BLOCK, BLOCK), 1)
    ).astype(F32)
    run = dot(decay[...], tri, TN, lax.Precision.HIGHEST)
    steps = dot(step[...], eye, TN, lax.Precision.HIGHEST)
    low = jnp.concatenate([run[:HALF], steps[:HALF]], axis=0)
    high = jnp.concatenate([run[HALF:], steps[HALF:]], axis=0)
    rows_keep[...] = jnp.where(core == 0, low, high)
    send[0:BLOCK, :512] = jnp.where(core == 0, x[:, 512:], x[:, :512])
    send[0:BLOCK, 512:768] = b[...]
    send[0:BLOCK, 768:1024] = c[...]
    send[0:BLOCK, 1024:] = q[...]
    send[BLOCK:, 384:] = jnp.zeros((16, 1152), BF16)
    for i, piece in enumerate(split3(jnp.where(core == 0, high, low))):
        send[BLOCK:, i * 128 : (i + 1) * 128] = piece


def received_rows(received):
    tail = received[BLOCK:, 0:384].astype(F32)
    return tail[:, 0:128] + tail[:, 128:256] + tail[:, 256:384]


def columns_of(rows):
    padded = jnp.concatenate([rows, jnp.zeros((BLOCK - rows.shape[0], BLOCK), F32)], axis=0)
    return padded.T


def spread(cols, first):
    lane = lax.broadcasted_iota(jnp.int32, (BLOCK, 128), 1)
    return jnp.where(lane < MDIM, cols[:, first : first + 1], cols[:, first + 1 : first + 2])


def first_place(head):
    row, lane = 2 * BLOCK + head % 4 * MDIM, head // 4 * SDIM
    return (slice(row, row + MDIM), slice(lane, lane + SDIM))


def states_kernel(
    place, x, b, c, rows_own, received, gain, q, sums, payload, kept, q_pair, sums_out
):
    core = place[2]
    sums_out[...] = sums[...]
    q_pair[:, :512] = q[...]
    q_pair[:, 512:] = received[0:BLOCK, 1024:]
    causal = lax.broadcasted_iota(jnp.int32, (BLOCK, BLOCK), 0) >= lax.broadcasted_iota(
        jnp.int32, (BLOCK, BLOCK), 1
    )
    x_own = jnp.where(core == 0, x[:, :512], x[:, 512:])
    blocks = (
        (x_own, b[...], c[...], rows_own[...]),
        (
            received[0:BLOCK, :512],
            received[0:BLOCK, 512:768],
            received[0:BLOCK, 768:1024],
            received_rows(received),
        ),
    )
    gains = gain[...]
    states = []
    totals = []
    for which, (xs, bs, cs, rows) in enumerate(blocks):
        cols = columns_of(rows)
        mixed = dot(cs, bs, NT)
        ends = rows[:, BLOCK - 1 : BLOCK]
        totals.append(ends)
        scaled = []
        for pair in range(HALF // 2):
            parts = []
            for head in (2 * pair, 2 * pair + 1):
                gap = cols[:, head : head + 1] - rows[head : head + 1, :]
                grown = jnp.exp(jnp.where(causal, gap, LOW))
                weight = (grown * mixed * rows[HALF + head : HALF + head + 1, :]).astype(BF16)
                parts.append(dot(weight, xs[:, head * MDIM : (head + 1) * MDIM]))
            lanes = slice(pair * 128, (pair + 1) * 128)
            wide = xs[:, lanes].astype(F32)
            inside = jnp.concatenate(parts, axis=1) + gains[:, lanes] * wide
            kept[which * BLOCK : (which + 1) * BLOCK, lanes] = inside.astype(BF16)
            lane = lax.broadcasted_iota(jnp.int32, (1, 128), 1)
            end = jnp.where(lane < MDIM, ends[2 * pair : 2 * pair + 1], ends[2 * pair + 1 : 2 * pair + 2])
            to_end = jnp.exp(end - spread(cols, 2 * pair)) * spread(cols, HALF + 2 * pair)
            scaled.append((to_end * wide).astype(BF16))
        states.append(dot(jnp.concatenate(scaled, axis=1), bs, TN))
    lengths = totals[0] + totals[1]
    for head in range(HALF):
        rows = slice(head * MDIM, (head + 1) * MDIM)
        own, other = states[0][rows], states[1][rows]
        gain_own = jnp.exp(totals[0][head : head + 1])
        gain_other = jnp.exp(totals[1][head : head + 1])
        kept[first_place(head)] = jnp.where(core == 0, own, other).astype(BF16)
        joint = jnp.where(core == 0, gain_other * own + other, gain_own * other + own).astype(BF16)
        hi, mid, lo = split3(jnp.broadcast_to(lengths[head : head + 1], (8, 128)))
        tag = lax.broadcasted_iota(jnp.int32, (8, 128), 0)
        total = jnp.where(tag == 0, hi.astype(F32), jnp.where(tag == 1, mid.astype(F32), lo.astype(F32)))
        for part in range(4):
            chunk = head * 4 + part
            payload[chunk, 0:16, :] = joint[part * 16 : (part + 1) * 16, :128]
            payload[chunk, 16:32, :] = joint[part * 16 : (part + 1) * 16, 128:]
            payload[chunk, 32:40, :] = total.astype(BF16)


def scan_kernel(arrived, sums, after, entering, sums_out):
    sums_out[...] = sums[...]
    state = jnp.zeros((32, 128), F32)
    for chip in range(CHIPS):
        entering[chip] = state.astype(BF16)
        tail = arrived[chip, 32:40, :].astype(F32)
        gain = jnp.exp(tail[0:1] + tail[1:2] + tail[2:3])
        state = gain * state + arrived[chip, 0:32, :].astype(F32)


def finish_kernel(place, entering, c, received, rows_own, sums, kept, parts, own, other, sums_out):
    core = place[2]
    sums_out[...] = sums[...]
    other[:, 512:] = parts[:, WIDE:]
    state_low = entering[:, 0:16, :].reshape(512, 128)
    state_high = entering[:, 16:32, :].reshape(512, 128)
    rows_mine, rows_theirs = rows_own[...], received_rows(received)
    first_total = jnp.where(core == 0, rows_mine[:HALF], rows_theirs[:HALF])[:, BLOCK - 1 : BLOCK]
    gain = jnp.exp(first_total)
    low, high = [], []
    for head in range(HALF):
        rows = slice(head * MDIM, (head + 1) * MDIM)
        first = kept[first_place(head)].astype(F32)
        low.append(gain[head : head + 1] * state_low[rows].astype(F32) + first[:, :128])
        high.append(gain[head : head + 1] * state_high[rows].astype(F32) + first[:, 128:])
    next_low = jnp.concatenate(low, axis=0).astype(BF16)
    next_high = jnp.concatenate(high, axis=0).astype(BF16)
    own_low = jnp.where(core == 0, state_low, next_low)
    own_high = jnp.where(core == 0, state_high, next_high)
    other_low = jnp.where(core == 0, next_low, state_low)
    other_high = jnp.where(core == 0, next_high, state_high)
    for which, (cs, at_low, at_high, rows, out) in enumerate(
        (
            (c[...], own_low, own_high, rows_mine, own),
            (received[0:BLOCK, 768:1024], other_low, other_high, rows_theirs, other),
        )
    ):
        carried = dot(cs[:, :128], at_low, NT) + dot(cs[:, 128:], at_high, NT)
        cols = jnp.exp(columns_of(rows))
        for pair in range(HALF // 2):
            lanes = slice(pair * 128, (pair + 1) * 128)
            out[:, lanes] = (
                kept[which * BLOCK : (which + 1) * BLOCK, lanes].astype(F32)
                + spread(cols, 2 * pair) * carried[:, lanes]
            ).astype(BF16)


SCALE = HEAD_SIZE ** (-0.5)
SCALE2 = SCALE * math.log2(math.e)
ROWS = 2 * 4 * BLOCK
TAIL = 128


def copies_kernel(keys, values, out, both, done):
    into = [
        pltpu.make_async_copy(keys, both.at[:, pl.ds(0, HEAD_SIZE)], done.at[0]),
        pltpu.make_async_copy(values, both.at[:, pl.ds(HEAD_SIZE, HEAD_SIZE)], done.at[1]),
    ]
    for copy in into:
        copy.start()
    for copy in into:
        copy.wait()
    away = [pltpu.make_async_copy(both, out.at[i], done.at[2 + i]) for i in range(NY)]
    for copy in away:
        copy.start()
    for copy in away:
        copy.wait()


WIDE = 512 + TAIL


def marked(tail, h, top, amount):
    lane = lax.broadcasted_iota(jnp.int32, (BLOCK, TAIL), 1)
    for i, piece in enumerate(split3(top) + split3(amount)):
        tail = jnp.where(lane == h * 6 + i, piece.astype(F32), tail)
    return tail


def part_of(ref, start, h):
    t = ref[:, start + 512 : start + WIDE].astype(F32)
    at = h * 6
    top = t[:, at : at + 1] + t[:, at + 1 : at + 2] + t[:, at + 2 : at + 3]
    amount = t[:, at + 3 : at + 4] + t[:, at + 4 : at + 5] + t[:, at + 5 : at + 6]
    return ref[:, start + h * 128 : start + (h + 1) * 128].astype(F32), top, amount


def combine(parts):
    highest = functools.reduce(jnp.maximum, [top for _, top, _ in parts])
    weights = [amount * jnp.exp(top - highest) for _, top, amount in parts]
    whole = sum(weights)
    scale = 1.0 / jnp.maximum(whole, 1e-30)
    return sum((w * scale) * mean for w, (mean, _, _) in zip(weights, parts)), highest, whole


def absorb(q, acc, top, kv, count, number, query_core=None, row=None, core=None):
    both = kv[0:count].reshape(count * BLOCK, 2 * HEAD_SIZE)
    keys = both[:, :HEAD_SIZE]
    values = jnp.concatenate([both[:, HEAD_SIZE:], jnp.ones((count * BLOCK, 128), BF16)], axis=1)
    place_of_key = lax.broadcasted_iota(jnp.int32, (1, count * BLOCK), 1)
    hidden = jnp.where(place_of_key < number * BLOCK, 0.0, 2 * LOW)
    for piece in range(ROWS // BLOCK):
        rows = slice(piece * BLOCK, (piece + 1) * BLOCK)
        block, h = piece // 4, piece % 4
        at = block * 512 + h * 128
        scores = dot(q[:, at : at + 128], keys, NT)
        if query_core is not None:
            theirs = query_core[block]
            sub = lax.broadcasted_iota(jnp.int32, (BLOCK, count * BLOCK), 0)
            lane = lax.broadcasted_iota(jnp.int32, (BLOCK, count * BLOCK), 1)
            limit = row * BLOCK + jnp.where(core == theirs, sub, jnp.where(core < theirs, BLOCK - 1, -1))
            scores = jnp.where(lane <= limit, scores, 2 * LOW)
            highest = jnp.maximum(jnp.max(scores, axis=1, keepdims=True), LOW)
            weights = jnp.exp2((scores - highest) * SCALE2).astype(BF16)
            top[rows, :] = jnp.broadcast_to(highest, (BLOCK, 128))
            acc[rows, :] = dot(weights, values)
        else:
            scores = scores + hidden
            old = top[rows, :]
            highest = jnp.maximum(old, jnp.max(scores, axis=1, keepdims=True))
            weights = jnp.exp2((scores - highest[:, 0:1]) * SCALE2).astype(BF16)
            factor = jnp.exp2((old - highest) * SCALE2)
            top[rows, :] = highest
            acc[rows, :] = acc[rows, :] * jnp.concatenate([factor, factor], axis=1) + dot(weights, values)


def near_kernel(place, q, kv, out, marks, token, acc, top):
    row, core = place[0], place[2]
    token[...] = jnp.zeros((1, 128), F32)
    for count, here in ((8, row >= 4), (4, row < 4)):

        @pl.when(here)
        def _():
            absorb(q, acc, top, kv, count, 0, (core, 1 - core), row, core)

    out[...] = acc[:, 0:128]
    lane = lax.broadcasted_iota(jnp.int32, (BLOCK, 128), 1)
    both = jnp.zeros((BLOCK, 128), F32)
    for piece in range(ROWS // BLOCK):
        rows = slice(piece * BLOCK, (piece + 1) * BLOCK)
        both = jnp.where(lane == 2 * piece, top[rows, :], both)
        both = jnp.where(lane == 2 * piece + 1, acc[rows, 128:], both)
    marks[...] = both


def far_kernel(place, q, left, right, far, before, marks, sums, parts, sums_out, acc, top):
    row, col = place[0], place[1]
    sums_out[...] = sums[...]
    for piece in range(ROWS // BLOCK):
        rows = slice(piece * BLOCK, (piece + 1) * BLOCK)
        top[rows, :] = jnp.broadcast_to(marks[:, 2 * piece : 2 * piece + 1], (BLOCK, 128))
        acc[rows, 0:128] = before[rows, :]
        acc[rows, 128:] = jnp.broadcast_to(marks[:, 2 * piece + 1 : 2 * piece + 2], (BLOCK, 128))
    for kv, step in ((left, 3), (right, 1), (far, 2)):
        number = row + (lax.rem(col + step, NX) < col).astype(jnp.int32)
        for count, here in ((8, number > 4), (4, (number > 0) & (number <= 4))):

            @pl.when(here)
            def _():
                absorb(q, acc, top, kv, count, number)

    for block in range(2):
        start = block * WIDE
        tail = jnp.zeros((BLOCK, TAIL), F32)
        for h in range(4):
            rows = slice((block * 4 + h) * BLOCK, (block * 4 + h + 1) * BLOCK)
            amount = acc[rows, 128:]
            mean = acc[rows, 0:128] / jnp.maximum(amount, 1e-30)
            parts[:, start + h * 128 : start + (h + 1) * 128] = mean.astype(BF16)
            tail = marked(tail, h, top[rows, :] * SCALE, amount)
        parts[:, start + 512 : start + WIDE] = tail.astype(BF16)


def merge_kernel(place, parts, own, received, mamba_out, attn_out):
    core = place[2]
    mine, theirs = own[...], received[:, :512]
    mamba_out[:, :512] = jnp.where(core == 0, mine, theirs)
    mamba_out[:, 512:] = jnp.where(core == 0, theirs, mine)
    for h in range(4):
        mean, _, _ = combine([part_of(parts, 0, h), part_of(received, 512, h)])
        attn_out[:, h * 128 : (h + 1) * 128] = mean.astype(BF16)


def shift(array, axis, size, by):
    return lax.ppermute(array, axis, [(i, (i + by) % size) for i in range(size)])


def swap(array, axis, size, mask):
    return lax.ppermute(array, axis, [(i, i ^ mask) for i in range(size)])


def on_device(
    mamba_input,
    step,
    log_decay,
    state_in,
    state_out,
    skip_gain,
    queries,
    keys,
    values,
    residual,
    norm_gain,
):
    core = lax.axis_index("c")
    place = jnp.stack([lax.axis_index("y"), lax.axis_index("x"), core]).astype(jnp.int32)
    b_in = state_in.reshape(BLOCK, SDIM)
    c_in = state_out.reshape(BLOCK, SDIM)

    anywhere = pl.BlockSpec(memory_space=pl.ANY)
    copies = pl.pallas_call(
        copies_kernel,
        out_shape=shape((NY, BLOCK, 2 * HEAD_SIZE), BF16),
        in_specs=[anywhere, anywhere],
        out_specs=anywhere,
        scratch_shapes=[pltpu.VMEM((BLOCK, 2 * HEAD_SIZE), BF16), pltpu.SemaphoreType.DMA((2 + NY,))],
        cost_estimate=cost(1),
    )(keys, values)
    kv_here = lax.all_to_all(copies, "y", 0, 0, tiled=True)

    send, rows_own = call(
        prepare_kernel,
        (shape((BLOCK + 16, 1536), BF16), shape((16, BLOCK), F32)),
        cost=cost(1),
        inputs=6,
        after=1,
    )(place, mamba_input, step, log_decay, b_in, c_in, queries, copies)
    received = swap(send, "c", NC, 1)

    widened = residual.astype(F32)
    sums = jnp.sum(widened * widened, axis=1).reshape(1, BLOCK)
    sums = sums + swap(sums, "z", NZ, 1)

    gains = jnp.repeat(lax.dynamic_slice(skip_gain, (core * HALF,), (HALF,)), MDIM)[None, :]
    payload, kept, q_near, sums = call(
        states_kernel,
        (
            shape((CHIPS, 40, 128), BF16),
            shape((512, 512), BF16),
            shape((BLOCK, 1024), BF16),
            shape((1, BLOCK), F32),
        ),
        cost=cost(3),
        inputs=8,
    )(place, mamba_input, b_in, c_in, rows_own, received, gains, queries, sums)
    arrived = lax.all_to_all(payload, ("y", "x"), 0, 0, tiled=True)

    kv_far = shift(kv_here, "x", NX, 2)
    kv_left = shift(kv_here, "x", NX, 1)
    kv_right = shift(kv_here, "x", NX, -1)
    wide = [pltpu.VMEM((ROWS, 256), F32), pltpu.VMEM((ROWS, 128), F32)]
    near, marks, token = call(
        near_kernel,
        (shape((ROWS, 128), F32), shape((BLOCK, 128), F32), shape((1, 128), F32)),
        scratch=wide,
        cost=cost(0.05),
        inputs=2,
    )(place, q_near, kv_here)

    entering, sums = call(
        scan_kernel,
        (shape((CHIPS, 32, 128), BF16), shape((1, BLOCK), F32)),
        cost=cost(1),
        scalars=0,
        inputs=3,
    )(arrived, sums, token)
    returned = lax.all_to_all(entering, ("y", "x"), 0, 0, tiled=True)

    sums = sums + swap(sums, "z", NZ, 4)
    parts, sums = call(
        far_kernel,
        (shape((BLOCK, 2 * WIDE), BF16), shape((1, BLOCK), F32)),
        scratch=wide,
        cost=cost(0.05),
        inputs=7,
    )(place, q_near, kv_left, kv_right, kv_far, near, marks, sums)
    own, other, sums = call(
        finish_kernel,
        (shape((BLOCK, 512), BF16), shape((BLOCK, 1024 + TAIL), BF16), shape((1, BLOCK), F32)),
        cost=cost(0.05),
        inputs=7,
    )(place, returned, c_in, received, rows_own, sums, kept, parts)
    theirs = swap(other, "c", NC, 1)
    sums = sums + swap(sums, "z", NZ, 2)
    scale = lax.rsqrt(sums.reshape(BLOCK, 1) / D + 1e-05)
    normed = (widened * scale * norm_gain[None, :]).astype(BF16)

    mamba_out, attn_out = call(
        merge_kernel,
        (shape((BLOCK, 1024), BF16), shape((BLOCK, 512), BF16)),
        cost=cost(2),
        inputs=3,
    )(place, parts, own, theirs)
    return mamba_out, attn_out, normed


def solution(mesh):
    grid = Mesh(mesh.devices.reshape(NY, NX, NC, NZ), ("y", "x", "c", "z"))
    ctx = ("y", "x", "c")
    placed = (
        P(ctx, "z"),
        P(ctx, "z"),
        P(ctx, "z"),
        P(ctx, "z", None),
        P(ctx, "z", None),
        P("z"),
        P(ctx, "z"),
        P(ctx, "z"),
        P(ctx, "z"),
        P(ctx, "z"),
        P("z"),
    )
    return jax.shard_map(
        on_device,
        mesh=grid,
        in_specs=placed,
        out_specs=(P(ctx, "z"), P(ctx, "z"), P(ctx, "z")),
        check_vma=False,
    )
```
